32 devices in a mesh: rows: 4 (over x, core), cols: 8 (over z, y).
Axes of the slice: x: 2, y: 2, z: 4, core: 2. Of those that a mesh axis runs over, the one named last changes fastest.
Arguments:
- expression: float32 [4096, 1024], P(('rows', 'cols')), may hold values from -10 to 10
- pivots: int32 [512], replicated, may hold values from 0 to 4095
- degrees: int32 [4096], replicated, may hold values from 256 to 8191
Outputs:
- correlation: float32 [4096, 4096], P('rows', 'cols')
The draws below stay inside these ranges and needn't reach their ends.
All inputs are finite; a program needn't handle non-finite values.
Results may differ from the reference program's by a relative error of at most 0.00042.
Values may be sent and summed in bfloat16 or wider, within the bound.
No kernel may reach another device: no remote copies, remote signals or barrier semaphores. Data moves between devices by JAX's collectives and lax.ppermute only.
A program may use at most 64 MiB of HBM per device.

```python
import jax
import jax.numpy as jnp
from jax import lax

S = 1024
P_SIZE = 512
G_DEV = 128
G = 4096
N_ROWS = 4
N_COLS = 8


def draw_expression(key, part):
    programs_count = 256
    subkeys = jax.random.split(jax.random.fold_in(key, 17), 7)
    programs = jnp.clip(jax.random.normal(subkeys[0], (programs_count, S), jnp.float32), -4.0, 4.0)
    noise_part = jnp.clip(jax.random.normal(subkeys[6], (G, S), jnp.float32), -4.0, 4.0)
    primary = jax.random.randint(subkeys[1], (G,), 0, programs_count)
    secondary = (primary + jax.random.randint(subkeys[2], (G,), 1, programs_count)) % programs_count
    signs = (jax.random.randint(subkeys[3], (G, 2), 0, 2) * 2 - 1).astype(jnp.float32)
    lead_load = jax.random.uniform(subkeys[4], (G,), jnp.float32, 0.6, 0.85)
    side_load = jax.random.uniform(subkeys[5], (G,), jnp.float32, 0.25, 0.45)
    rest_load = jnp.sqrt(1.0 - lead_load * lead_load - side_load * side_load)
    values = (lead_load * signs[:, 0])[:, None] * programs[primary]
    values = values + (side_load * signs[:, 1])[:, None] * programs[secondary]
    values = values + rest_load[:, None] * noise_part
    return values.astype(jnp.float32)


def with_ends(array, key, low, high):
    longest = array.shape.index(max(array.shape))
    spots = []
    for shift in (0, 1):
        where = [jax.random.randint(jax.random.fold_in(key, axis), (), 0, length) for axis, length in enumerate(array.shape)]
        where[longest] = (where[longest] + shift) % array.shape[longest]
        spots.append(tuple(where))
    return array.at[spots[0]].set(low).at[spots[1]].set(high)


def setup_inputs(seed: int = 0) -> dict:
    streams_of = jax.random.split(jax.random.key(seed), 4)
    expression = draw_expression(jax.random.fold_in(streams_of[3], 71), 0)
    pivots = with_ends(jax.random.randint(streams_of[1], (P_SIZE,), 0, G), jax.random.fold_in(streams_of[1], 1), 0, G - 1).astype(jnp.int32)
    degrees = with_ends(jax.random.randint(streams_of[2], (G,), 256, 8192), jax.random.fold_in(streams_of[2], 1), 256, 8191).astype(jnp.int32)
    return {"expression": expression, "pivots": pivots, "degrees": degrees}


def standard(expression):
    centered = expression - lax.optimization_barrier(jnp.mean(expression, axis=1, keepdims=True))
    spread = lax.optimization_barrier(jnp.mean(centered * centered, axis=1, keepdims=True))
    return (centered * lax.rsqrt(spread + 1e-06)).astype(jnp.bfloat16)

def adjacency(left, right):
    corr = jnp.dot(left, right.T, preferred_element_type=jnp.float32) / S
    return ((1.0 + corr) * 0.5) ** 6

def reference(expression, pivots, degrees):
    zrows = standard(expression)
    zpiv = zrows[pivots]
    piv_adj = adjacency(zrows, zpiv).astype(jnp.bfloat16)
    order = jnp.arange(G, dtype=jnp.int32).reshape(N_ROWS, N_COLS, G_DEV).transpose(1, 0, 2).reshape(-1)
    zcol = zrows[order]
    acol = piv_adj[order]
    scale = degrees.astype(jnp.float32) * (1.0 / 1024.0)
    kcol = scale[order]
    blocks = G // 1024 if G % 1024 == 0 else G // G_DEV

    def one_block(index):
        width = G // blocks
        zr = lax.dynamic_slice_in_dim(zrows, index * width, width, 0)
        ar = lax.dynamic_slice_in_dim(piv_adj, index * width, width, 0)
        kr = lax.dynamic_slice_in_dim(scale, index * width, width, 0)
        direct = adjacency(zr, zcol)
        shared = jnp.dot(ar, acol.T, preferred_element_type=jnp.float32)
        denom = jnp.minimum(kr[:, None], kcol[None, :]) + 1.0 - direct
        return (shared + direct) / denom
    result = lax.map(one_block, jnp.arange(blocks, dtype=jnp.int32))
    return result.reshape(G, G)
```

```python
import functools

import jax
import jax.numpy as jnp
from jax import lax
from jax.experimental import pallas as pl
from jax.experimental.pallas import tpu as pltpu
from jax.sharding import PartitionSpec as P

VMEM = pl.BlockSpec(memory_space=pltpu.VMEM)
SMEM = pl.BlockSpec(memory_space=pltpu.SMEM)
ANY = pl.BlockSpec(memory_space=pl.ANY)
LIMIT = 48 * 1024 * 1024


def params():
    return pltpu.CompilerParams(vmem_limit_bytes=LIMIT)


def dot_t(left, right):
    return lax.dot_general(
        left, right, (((1,), (1,)), ((), ())), preferred_element_type=jnp.float32
    )


def power6(product, samples):
    half = (1.0 + product * (1.0 / samples)) * 0.5
    square = half * half
    return square * square * square


def standard_kernel(x_ref, z_ref, za_ref, zb_ref):
    x = x_ref[...]
    centered = x - jnp.mean(x, axis=1, keepdims=True)
    spread = jnp.mean(centered * centered, axis=1, keepdims=True)
    z = (centered * lax.rsqrt(spread + 1e-06)).astype(jnp.bfloat16)
    z_ref[...] = z
    wa = za_ref.shape[1]
    za_ref[...] = z[:, :wa]
    zb_ref[...] = z[:, wa:]


def select_kernel(n, hot_ref, *refs):
    shards, (mine_ref, theirs_ref) = refs[:n], refs[n:]
    half = mine_ref.shape[0]
    genes = jnp.concatenate([s[...] for s in shards], axis=0)
    for out, at in ((mine_ref, 0), (theirs_ref, half)):
        out[...] = jnp.dot(
            hot_ref[at : at + half, :], genes, preferred_element_type=jnp.float32
        ).astype(jnp.bfloat16)


def final_kernel(n, m, cols_ref, kr_ref, kc_ref, *refs):
    refs = list(refs)
    take = lambda count: [refs.pop(0) for _ in range(count)]
    za, zb, pieces, pa, pb = take(n), take(n), take(m), take(2), take(2)
    out_ref, zr, zc, zp, stage, sems = refs
    local, samples = pieces[0].shape
    wa = za[0].shape[1]
    half = pa[0].shape[0]
    for j in range(n):
        at = pl.ds(pl.multiple_of(cols_ref[j] * local, local), local)
        zr[at, :wa] = za[j][...]
        zr[at, wa:] = zb[j][...]
    for i in range(m):
        at = pl.ds(pl.multiple_of(cols_ref[n + i] * local, local), local)
        zc[at, :] = pieces[i][...]
    for i in range(2):
        zp[i * half : (i + 1) * half, :wa] = pa[i][...]
        zp[i * half : (i + 1) * half, wa:] = pb[i][...]
    acol = power6(dot_t(zc[...], zp[...]), samples).astype(jnp.bfloat16)
    block = 2 * local
    copies = []
    for b in range(n * local // block):
        rows = slice(b * block, (b + 1) * block)
        arow = power6(dot_t(zr[rows, :], zp[...]), samples).astype(jnp.bfloat16)
        direct = power6(dot_t(zr[rows, :], zc[...]), samples)
        shared = dot_t(arow, acol)
        denom = jnp.minimum(kr_ref[rows, :], kc_ref[...]) + 1.0 - direct
        stage[rows, :] = (shared + direct) / denom
        copy = pltpu.make_async_copy(
            stage.at[rows, :], out_ref.at[rows, :], sems.at[b]
        )
        copy.start()
        copies.append(copy)
    for copy in copies:
        copy.wait()


def per_device(expression, pivots, degrees):
    n_rows = lax.axis_size("rows")
    n = lax.axis_size("cols")
    r = lax.axis_index("rows")
    c = lax.axis_index("cols")
    local, samples = expression.shape
    wa = samples // 2
    wb = samples - wa
    bf16 = jnp.bfloat16

    z, za, zb = pl.pallas_call(
        standard_kernel,
        out_shape=[
            jax.ShapeDtypeStruct((local, samples), bf16),
            jax.ShapeDtypeStruct((local, wa), bf16),
            jax.ShapeDtypeStruct((local, wb), bf16),
        ],
        in_specs=[VMEM],
        out_specs=[VMEM] * 3,
        compiler_params=params(),
        name="standardize",
    )(expression)

    order = list(range(0, n, 2)) + list(range(n - 1, 0, -2))
    forward = [(order[k], order[(k + 1) % n]) for k in range(n)]
    backward = [(b, a) for a, b in forward]
    flip = lambda v, mask: lax.ppermute(
        v, "rows", [(i, i ^ mask) for i in range(n_rows)]
    )

    offsets = [0]
    for s in range(1, n // 2 + 1):
        offsets += [-s, s] if s < n // 2 else [s]
    fa, ba, fb, bb = za, za, zb, zb
    list_a, list_b = [za], [zb]
    pieces, masks = [z], [0]
    for s in range(1, n // 2 + 1):
        last = s == n // 2
        fa = lax.ppermute(fa, "cols", forward)
        list_a.append(fa)
        if not last:
            ba = lax.ppermute(ba, "cols", backward)
            list_a.append(ba)
            fb = lax.ppermute(fb, "cols", forward)
            list_b.append(fb)
        bb = lax.ppermute(bb, "cols", backward)
        list_b.append(bb)
        if s == 1:
            mask = n_rows // 2
            while mask:
                pieces += [flip(p, mask) for p in pieces]
                masks += [q ^ mask for q in masks]
                mask //= 2

    place = jnp.where(c % 2 == 0, c // 2, n - 1 - c // 2)
    spots = (place + jnp.array(offsets, jnp.int32)) % n
    columns = jnp.where(spots < n // 2, 2 * spots, 2 * (n - 1 - spots) + 1)
    ids = ((r * n + columns)[:, None] * local + jnp.arange(local, dtype=jnp.int32)).reshape(-1)
    half = pivots.shape[0] // 2
    side = r % 2
    split = pivots.reshape(2, half)
    ordered = jnp.concatenate(
        [
            lax.dynamic_index_in_dim(split, side, 0, False),
            lax.dynamic_index_in_dim(split, 1 - side, 0, False),
        ]
    )
    hot = (ordered[:, None] == ids[None, :]).astype(bf16)

    def pivot_rows(shards):
        width = shards[0].shape[1]
        mine, theirs = pl.pallas_call(
            functools.partial(select_kernel, n),
            out_shape=[jax.ShapeDtypeStruct((half, width), bf16)] * 2,
            in_specs=[VMEM] * (n + 1),
            out_specs=[VMEM] * 2,
            compiler_params=params(),
            name="select",
        )(hot, *shards)
        total = mine + flip(theirs, 1)
        mask = 2
        while mask < n_rows:
            total = total + flip(total, mask)
            mask *= 2
        return total, flip(total, 1)

    pa = pivot_rows(list_a)
    pb = pivot_rows(list_b)

    scale = degrees.astype(jnp.float32) * (1.0 / 1024.0)
    kc = lax.dynamic_index_in_dim(scale.reshape(n_rows, n, local), c, 1, False).reshape(1, -1)
    height = n * local
    kr = lax.dynamic_slice_in_dim(scale, r * height, height, 0).reshape(-1, 1)
    where = jnp.concatenate([columns, jnp.array(masks, jnp.int32) ^ r])
    width = n_rows * local
    return pl.pallas_call(
        functools.partial(final_kernel, n, n_rows),
        out_shape=jax.ShapeDtypeStruct((height, width), jnp.float32),
        in_specs=[SMEM] + [VMEM] * (2 + 2 * n + n_rows + 4),
        out_specs=ANY,
        scratch_shapes=[
            pltpu.VMEM((height, samples), bf16),
            pltpu.VMEM((width, samples), bf16),
            pltpu.VMEM((2 * half, samples), bf16),
            pltpu.VMEM((height, width), jnp.float32),
            pltpu.SemaphoreType.DMA((n // 2,)),
        ],
        compiler_params=params(),
        name="final",
    )(where, kr, kc, *list_a, *list_b, *pieces, *pa, *pb)


def solution(mesh):
    in_specs = (P(("rows", "cols"), None), P(), P())
    out_specs = P("rows", "cols")
    return jax.shard_map(
        per_device, mesh=mesh, in_specs=in_specs, out_specs=out_specs, check_vma=False
    )
```

```python
import functools

import jax
import jax.numpy as jnp
from jax import lax
from jax.experimental import pallas as pl
from jax.experimental.pallas import tpu as pltpu
from jax.sharding import PartitionSpec as P

VMEM = pl.BlockSpec(memory_space=pltpu.VMEM)
SMEM = pl.BlockSpec(memory_space=pltpu.SMEM)
ANY = pl.BlockSpec(memory_space=pl.ANY)
MIB = 1024 * 1024


def params(mib):
    return pltpu.CompilerParams(vmem_limit_bytes=mib * MIB)


CHEAP = pl.CostEstimate(flops=1, bytes_accessed=1, transcendentals=0)


def dot_t(left, right):
    return lax.dot_general(
        left, right, (((1,), (1,)), ((), ())), preferred_element_type=jnp.float32
    )


def power6(product, samples):
    half = (1.0 + product * (1.0 / samples)) * 0.5
    square = half * half
    return square * square * square


def standard_kernel(x_ref, z_ref, za_ref, zb_ref):
    x = x_ref[...]
    centered = x - jnp.mean(x, axis=1, keepdims=True)
    spread = jnp.mean(centered * centered, axis=1, keepdims=True)
    z = (centered * lax.rsqrt(spread + 1e-06)).astype(jnp.bfloat16)
    z_ref[...] = z
    wa = za_ref.shape[1]
    za_ref[...] = z[:, :wa]
    zb_ref[...] = z[:, wa:]


def select_kernel(n, hot_ref, *refs):
    shards, (mine_ref, theirs_ref) = refs[:n], refs[n:]
    half = mine_ref.shape[0]
    genes = jnp.concatenate([s[...] for s in shards], axis=0)
    for out, at in ((mine_ref, 0), (theirs_ref, half)):
        out[...] = jnp.dot(
            hot_ref[at : at + half, :], genes, preferred_element_type=jnp.float32
        ).astype(jnp.bfloat16)


def direct_kernel(n, m, cols_ref, kr_ref, kc_ref, *refs):
    refs = list(refs)
    take = lambda count: [refs.pop(0) for _ in range(count)]
    za, zb, pieces = take(n), take(n), take(m)
    zr, zc, inverse, share = refs
    local, samples = pieces[0].shape
    wa = za[0].shape[1]
    for j in range(n):
        at = pl.ds(pl.multiple_of(cols_ref[j] * local, local), local)
        zr[at, :wa] = za[j][...]
        zr[at, wa:] = zb[j][...]
    for i in range(m):
        at = pl.ds(pl.multiple_of(cols_ref[n + i] * local, local), local)
        zc[at, :] = pieces[i][...]
    block = 2 * local
    for b in range(n * local // block):
        rows = slice(b * block, (b + 1) * block)
        direct = power6(dot_t(zr[rows, :], zc[...]), samples)
        inv = 1.0 / (jnp.minimum(kr_ref[rows, :], kc_ref[...]) + 1.0 - direct)
        inverse[rows, :] = inv
        share[rows, :] = direct * inv


def partial_kernel(zr, zc, near, far, row_part, col_part):
    wa = near.shape[1]
    zp = jnp.concatenate([near[...], far[...]], axis=0)
    row_part[...] = dot_t(zr[:, :wa], zp)
    col_part[...] = dot_t(zc[:, :wa], zp)


def final_kernel(zr, zc, near, far, row_part, col_part, inverse, share, out_ref, stage, sems):
    height, samples = zr.shape
    wa = samples - near.shape[1]
    zp = jnp.concatenate([near[...], far[...]], axis=0)
    acol = power6(col_part[...] + dot_t(zc[:, wa:], zp), samples).astype(jnp.bfloat16)
    count = sems.shape[0]
    block = height // count
    copies = []
    for b in range(count):
        rows = slice(b * block, (b + 1) * block)
        product = row_part[rows, :] + dot_t(zr[rows, wa:], zp)
        arow = power6(product, samples).astype(jnp.bfloat16)
        stage[rows, :] = dot_t(arow, acol) * inverse[rows, :] + share[rows, :]
        copy = pltpu.make_async_copy(
            stage.at[rows, :], out_ref.at[rows, :], sems.at[b]
        )
        copy.start()
        copies.append(copy)
    for copy in copies:
        copy.wait()


def add_kernel(left, right, out):
    out[...] = left[...] + right[...]


def add(left, right):
    return pl.pallas_call(
        add_kernel,
        out_shape=jax.ShapeDtypeStruct(left.shape, left.dtype),
        in_specs=[VMEM] * 2,
        out_specs=VMEM,
        compiler_params=params(4),
        cost_estimate=CHEAP,
        name="add",
    )(left, right)


def per_device(expression, pivots, degrees):
    n_rows = lax.axis_size("rows")
    n = lax.axis_size("cols")
    r = lax.axis_index("rows")
    c = lax.axis_index("cols")
    local, samples = expression.shape
    wa = samples // 2
    wb = samples - wa
    bf16 = jnp.bfloat16

    z, za, zb = pl.pallas_call(
        standard_kernel,
        out_shape=[
            jax.ShapeDtypeStruct((local, samples), bf16),
            jax.ShapeDtypeStruct((local, wa), bf16),
            jax.ShapeDtypeStruct((local, wb), bf16),
        ],
        in_specs=[VMEM],
        out_specs=[VMEM] * 3,
        compiler_params=params(8),
        name="standardize",
    )(expression)

    order = list(range(0, n, 2)) + list(range(n - 1, 0, -2))
    forward = [(order[k], order[(k + 1) % n]) for k in range(n)]
    backward = [(b, a) for a, b in forward]
    flip = lambda v, mask: lax.ppermute(
        v, "rows", [(i, i ^ mask) for i in range(n_rows)]
    )

    offsets = [0]
    for s in range(1, n // 2 + 1):
        offsets += [-s, s] if s < n // 2 else [s]
    fa, ba, fb, bb = za, za, zb, zb
    list_a, list_b = [za], [zb]
    top = n_rows // 2
    across = flip(z, top)
    for s in range(1, n // 2 + 1):
        last = s == n // 2
        if s == n // 2 - 1:
            fa, across = lax.optimization_barrier((fa, across))
        fa = lax.ppermute(fa, "cols", forward)
        list_a.append(fa)
        if not last:
            ba = lax.ppermute(ba, "cols", backward)
            list_a.append(ba)
            fb = lax.ppermute(fb, "cols", forward)
            list_b.append(fb)
        bb = lax.ppermute(bb, "cols", backward)
        list_b.append(bb)

    place = jnp.where(c % 2 == 0, c // 2, n - 1 - c // 2)
    spots = (place + jnp.array(offsets, jnp.int32)) % n
    columns = jnp.where(spots < n // 2, 2 * spots, 2 * (n - 1 - spots) + 1)
    ids = ((r * n + columns)[:, None] * local + jnp.arange(local, dtype=jnp.int32)).reshape(-1)
    half = pivots.shape[0] // 2
    side = r % 2
    split = pivots.reshape(2, half)
    ordered = jnp.concatenate(
        [
            lax.dynamic_index_in_dim(split, side, 0, False),
            lax.dynamic_index_in_dim(split, 1 - side, 0, False),
        ]
    )
    hot = (ordered[:, None] == ids[None, :]).astype(bf16)

    def pivot_sums(shards):
        width = shards[0].shape[1]
        mine, theirs = pl.pallas_call(
            functools.partial(select_kernel, n),
            out_shape=[jax.ShapeDtypeStruct((half, width), bf16)] * 2,
            in_specs=[VMEM] * (n + 1),
            out_specs=[VMEM] * 2,
            compiler_params=params(8),
            cost_estimate=CHEAP,
            name="select",
        )(hot, *shards)
        return add(mine, flip(theirs, 1))

    def spread(total, got):
        total = add(total, got)
        mask = 4
        while mask < n_rows:
            total = add(total, flip(total, mask))
            mask *= 2
        return total, flip(total, 1)

    sum_a = pivot_sums(list_a)
    got_a = flip(sum_a, 2)
    sum_b = pivot_sums(list_b)
    sum_b, z, across = lax.optimization_barrier((sum_b, z, across))
    got_b = flip(sum_b, 2)
    pieces, masks = [z, across], [0, top]
    mask = top // 2
    while mask:
        pieces += [flip(p, mask) for p in pieces]
        masks += [q ^ mask for q in masks]
        mask //= 2

    scale = degrees.astype(jnp.float32) * (1.0 / 1024.0)
    kc = lax.dynamic_index_in_dim(scale.reshape(n_rows, n, local), c, 1, False).reshape(1, -1)
    height = n * local
    kr = lax.dynamic_slice_in_dim(scale, r * height, height, 0).reshape(-1, 1)
    where = jnp.concatenate([columns, jnp.array(masks, jnp.int32) ^ r])
    width = n_rows * local
    f32 = jnp.float32
    shape = jax.ShapeDtypeStruct
    zr, zc, inverse, share = pl.pallas_call(
        functools.partial(direct_kernel, n, n_rows),
        out_shape=[
            shape((height, samples), bf16),
            shape((width, samples), bf16),
            shape((height, width), f32),
            shape((height, width), f32),
        ],
        in_specs=[SMEM] + [VMEM] * (2 + 2 * n + n_rows),
        out_specs=[VMEM] * 4,
        compiler_params=params(8),
        cost_estimate=CHEAP,
        name="direct",
    )(where, kr, kc, *list_a, *list_b, *pieces)
    got_a, got_b, zr, zc, inverse, share = lax.optimization_barrier((got_a, got_b, zr, zc, inverse, share))
    pa = spread(sum_a, got_a)
    row_part, col_part = pl.pallas_call(
        partial_kernel,
        out_shape=[shape((height, 2 * half), f32), shape((width, 2 * half), f32)],
        in_specs=[VMEM] * 4,
        out_specs=[VMEM] * 2,
        compiler_params=params(8),
        cost_estimate=CHEAP,
        name="partial",
    )(zr, zc, *pa)
    pb = spread(sum_b, got_b)
    return pl.pallas_call(
        final_kernel,
        out_shape=shape((height, width), f32),
        in_specs=[VMEM] * 8,
        out_specs=ANY,
        scratch_shapes=[pltpu.VMEM((height, width), f32), pltpu.SemaphoreType.DMA((n // 2,))],
        compiler_params=params(16),
        cost_estimate=CHEAP,
        name="final",
    )(zr, zc, *pb, row_part, col_part, inverse, share)


def solution(mesh):
    in_specs = (P(("rows", "cols"), None), P(), P())
    out_specs = P("rows", "cols")
    return jax.shard_map(
        per_device, mesh=mesh, in_specs=in_specs, out_specs=out_specs, check_vma=False
    )
```

```python
import functools

import jax
import jax.numpy as jnp
from jax import lax
from jax.experimental import pallas as pl
from jax.experimental.pallas import tpu as pltpu
from jax.sharding import PartitionSpec as P

VMEM = pl.BlockSpec(memory_space=pltpu.VMEM)
SMEM = pl.BlockSpec(memory_space=pltpu.SMEM)
ANY = pl.BlockSpec(memory_space=pl.ANY)
MIB = 1024 * 1024


def params(mib):
    return pltpu.CompilerParams(vmem_limit_bytes=mib * MIB)


CHEAP = pl.CostEstimate(flops=1, bytes_accessed=1, transcendentals=0)


def OUT(size, dtype):
    return pltpu.VMEM(size, dtype)


def dot_t(left, right):
    return lax.dot_general(
        left, right, (((1,), (1,)), ((), ())), preferred_element_type=jnp.float32
    )


def power6(product, samples):
    half = (1.0 + product * (1.0 / samples)) * 0.5
    square = half * half
    return square * square * square


def standard_kernel(x_ref, z_ref, za_ref, zb_ref):
    x = x_ref[...]
    centered = x - jnp.mean(x, axis=1, keepdims=True)
    spread = jnp.mean(centered * centered, axis=1, keepdims=True)
    z = (centered * lax.rsqrt(spread + 1e-06)).astype(jnp.bfloat16)
    z_ref[...] = z
    wa = za_ref.shape[1]
    za_ref[...] = z[:, :wa]
    zb_ref[...] = z[:, wa:]


def select_kernel(n, hot_ref, *refs):
    shards, (mine_ref, theirs_ref) = refs[:n], refs[n:]
    half = mine_ref.shape[0]
    genes = jnp.concatenate([s[...] for s in shards], axis=0)
    for out, at in ((mine_ref, 0), (theirs_ref, half)):
        out[...] = jnp.dot(
            hot_ref[at : at + half, :], genes, preferred_element_type=jnp.float32
        ).astype(jnp.bfloat16)


def direct_kernel(n, m, cols_ref, kr_ref, kc_ref, *refs):
    refs = list(refs)
    take = lambda count: [refs.pop(0) for _ in range(count)]
    za, zb, pieces = take(n), take(n), take(m)
    zr, zc, inverse, share = refs
    local, samples = pieces[0].shape
    wa = za[0].shape[1]
    for j in range(n):
        at = pl.ds(pl.multiple_of(cols_ref[j] * local, local), local)
        zr[at, :wa] = za[j][...]
        zr[at, wa:] = zb[j][...]
    for i in range(m):
        at = pl.ds(pl.multiple_of(cols_ref[n + i] * local, local), local)
        zc[at, :] = pieces[i][...]
    block = 2 * local
    for b in range(n * local // block):
        rows = slice(b * block, (b + 1) * block)
        direct = power6(dot_t(zr[rows, :], zc[...]), samples)
        inv = 1.0 / (jnp.minimum(kr_ref[rows, :], kc_ref[...]) + 1.0 - direct)
        inverse[rows, :] = inv
        share[rows, :] = direct * inv


def partial_kernel(zr, zc, near, far, row_part, col_part):
    wa = near.shape[1]
    zp = jnp.concatenate([near[...], far[...]], axis=0)
    row_part[...] = dot_t(zr[:, :wa], zp)
    col_part[...] = dot_t(zc[:, :wa], zp)


def final_kernel(zr, zc, near, far, row_part, col_part, inverse, share, out_ref, stage, sems):
    height, samples = zr.shape
    wa = samples - near.shape[1]
    zp = jnp.concatenate([near[...], far[...]], axis=0)
    acol = power6(col_part[...] + dot_t(zc[:, wa:], zp), samples).astype(jnp.bfloat16)
    count = sems.shape[0]
    block = height // count
    copies = []
    for b in range(count):
        rows = slice(b * block, (b + 1) * block)
        product = row_part[rows, :] + dot_t(zr[rows, wa:], zp)
        arow = power6(product, samples).astype(jnp.bfloat16)
        stage[rows, :] = dot_t(arow, acol) * inverse[rows, :] + share[rows, :]
        copy = pltpu.make_async_copy(
            stage.at[rows, :], out_ref.at[rows, :], sems.at[b]
        )
        copy.start()
        copies.append(copy)
    for copy in copies:
        copy.wait()


def add_kernel(left, right, out):
    out[...] = left[...] + right[...]


def add(left, right):
    return pl.pallas_call(
        add_kernel,
        out_shape=OUT(left.shape, left.dtype),
        in_specs=[VMEM] * 2,
        out_specs=VMEM,
        compiler_params=params(4),
        cost_estimate=CHEAP,
        name="add",
    )(left, right)


def sum_part_kernel(side_ref, left, right, both, part):
    total = left[...] + right[...]
    both[...] = total
    rows = part.shape[0]

    @pl.when(side_ref[0] == 0)
    def _():
        part[...] = total[:rows, :]

    @pl.when(side_ref[0] != 0)
    def _():
        part[...] = total[rows:, :]


def merge_kernel(side_ref, sum_a, got_a, sum_b, mine, mate, out_a, out_b):
    out_a[...] = sum_a[...] + got_a[...]
    rows = mine.shape[0]
    for side in range(2):
        first, second = (mine, mate) if side == 0 else (mate, mine)

        @pl.when(side_ref[0] == side)
        def _():
            out_b[:rows, :] = sum_b[:rows, :] + first[...]
            out_b[rows:, :] = sum_b[rows:, :] + second[...]


def per_device(expression, pivots, degrees):
    n_rows = lax.axis_size("rows")
    n = lax.axis_size("cols")
    r = lax.axis_index("rows")
    c = lax.axis_index("cols")
    local, samples = expression.shape
    wa = samples // 2
    wb = samples - wa
    bf16 = jnp.bfloat16

    z, za, zb = pl.pallas_call(
        standard_kernel,
        out_shape=[
            jax.ShapeDtypeStruct((local, samples), bf16),
            jax.ShapeDtypeStruct((local, wa), bf16),
            jax.ShapeDtypeStruct((local, wb), bf16),
        ],
        in_specs=[VMEM],
        out_specs=[VMEM] * 3,
        compiler_params=params(8),
        name="standardize",
    )(expression)

    order = list(range(0, n, 2)) + list(range(n - 1, 0, -2))
    forward = [(order[k], order[(k + 1) % n]) for k in range(n)]
    backward = [(b, a) for a, b in forward]
    flip = lambda v, mask: lax.ppermute(
        v, "rows", [(i, i ^ mask) for i in range(n_rows)]
    )

    offsets = [0]
    for s in range(1, n // 2 + 1):
        offsets += [-s, s] if s < n // 2 else [s]
    fa, ba, fb, bb = za, za, zb, zb
    list_a, list_b = [za], [zb]
    top = n_rows // 2
    across = flip(z, top)
    for s in range(1, n // 2 + 1):
        last = s == n // 2
        if s == n // 2 - 1:
            fa, across = lax.optimization_barrier((fa, across))
        fa = lax.ppermute(fa, "cols", forward)
        list_a.append(fa)
        if not last:
            ba = lax.ppermute(ba, "cols", backward)
            list_a.append(ba)
            fb = lax.ppermute(fb, "cols", forward)
            list_b.append(fb)
        bb = lax.ppermute(bb, "cols", backward)
        list_b.append(bb)

    place = jnp.where(c % 2 == 0, c // 2, n - 1 - c // 2)
    spots = (place + jnp.array(offsets, jnp.int32)) % n
    columns = jnp.where(spots < n // 2, 2 * spots, 2 * (n - 1 - spots) + 1)
    ids = ((r * n + columns)[:, None] * local + jnp.arange(local, dtype=jnp.int32)).reshape(-1)
    half = pivots.shape[0] // 2
    side = r % 2
    split = pivots.reshape(2, half)
    ordered = jnp.concatenate(
        [
            lax.dynamic_index_in_dim(split, side, 0, False),
            lax.dynamic_index_in_dim(split, 1 - side, 0, False),
        ]
    )
    hot = (ordered[:, None] == ids[None, :]).astype(bf16)

    def pivot_sums(shards):
        width = shards[0].shape[1]
        mine, theirs = pl.pallas_call(
            functools.partial(select_kernel, n),
            out_shape=[jax.ShapeDtypeStruct((half, width), bf16)] * 2,
            in_specs=[VMEM] * (n + 1),
            out_specs=[VMEM] * 2,
            compiler_params=params(8),
            cost_estimate=CHEAP,
            name="select",
        )(hot, *shards)
        return mine, flip(theirs, 1)

    parity = (c % 2).astype(jnp.int32).reshape(1)
    beside = [(k, k ^ 1) for k in range(n)]
    mine, theirs = pivot_sums(list_b)
    sum_b, part = pl.pallas_call(
        sum_part_kernel,
        out_shape=[OUT(mine.shape, bf16), OUT((half // 2, mine.shape[1]), bf16)],
        in_specs=[SMEM, VMEM, VMEM],
        out_specs=[VMEM] * 2,
        compiler_params=params(4),
        cost_estimate=CHEAP,
        name="sum",
    )(parity, mine, theirs)
    got_b = flip(part, top)
    sum_a = add(*pivot_sums(list_a))
    sum_a, z, across = lax.optimization_barrier((sum_a, z, across))
    got_a = flip(sum_a, top)
    mate_b = lax.ppermute(got_b, "cols", beside)
    pieces, masks = [z, across], [0, top]
    mask = top // 2
    while mask:
        pieces += [flip(p, mask) for p in pieces]
        masks += [q ^ mask for q in masks]
        mask //= 2

    scale = degrees.astype(jnp.float32) * (1.0 / 1024.0)
    kc = lax.dynamic_index_in_dim(scale.reshape(n_rows, n, local), c, 1, False).reshape(1, -1)
    height = n * local
    kr = lax.dynamic_slice_in_dim(scale, r * height, height, 0).reshape(-1, 1)
    where = jnp.concatenate([columns, jnp.array(masks, jnp.int32) ^ r])
    width = n_rows * local
    f32 = jnp.float32
    shape = jax.ShapeDtypeStruct
    zr, zc, inverse, share = pl.pallas_call(
        functools.partial(direct_kernel, n, n_rows),
        out_shape=[
            shape((height, samples), bf16),
            shape((width, samples), bf16),
            shape((height, width), f32),
            shape((height, width), f32),
        ],
        in_specs=[SMEM] + [VMEM] * (2 + 2 * n + n_rows),
        out_specs=[VMEM] * 4,
        compiler_params=params(8),
        cost_estimate=CHEAP,
        name="direct",
    )(where, kr, kc, *list_a, *list_b, *pieces)
    got_a, got_b, zr, zc, inverse, share, mate_b = lax.optimization_barrier(
        (got_a, got_b, zr, zc, inverse, share, mate_b)
    )
    total_a, total_b = pl.pallas_call(
        merge_kernel,
        out_shape=[OUT(sum_a.shape, bf16), OUT(sum_b.shape, bf16)],
        in_specs=[SMEM] + [VMEM] * 5,
        out_specs=[VMEM] * 2,
        compiler_params=params(4),
        cost_estimate=CHEAP,
        name="merge",
    )(parity, sum_a, got_a, sum_b, got_b, mate_b)
    pa, pb = (total_a, flip(total_a, 1)), (total_b, flip(total_b, 1))
    row_part, col_part = pl.pallas_call(
        partial_kernel,
        out_shape=[shape((height, 2 * half), f32), shape((width, 2 * half), f32)],
        in_specs=[VMEM] * 4,
        out_specs=[VMEM] * 2,
        compiler_params=params(8),
        cost_estimate=CHEAP,
        name="partial",
    )(zr, zc, *pa)
    return pl.pallas_call(
        final_kernel,
        out_shape=shape((height, width), f32),
        in_specs=[VMEM] * 8,
        out_specs=ANY,
        scratch_shapes=[pltpu.VMEM((height, width), f32), pltpu.SemaphoreType.DMA((n // 2,))],
        compiler_params=params(16),
        cost_estimate=CHEAP,
        name="final",
    )(zr, zc, *pb, row_part, col_part, inverse, share)


def solution(mesh):
    in_specs = (P(("rows", "cols"), None), P(), P())
    out_specs = P("rows", "cols")
    return jax.shard_map(
        per_device, mesh=mesh, in_specs=in_specs, out_specs=out_specs, check_vma=False
    )
```

```python
import functools

import jax
import jax.numpy as jnp
from jax import lax
from jax.experimental import pallas as pl
from jax.experimental.pallas import tpu as pltpu
from jax.sharding import PartitionSpec as P

VMEM = pl.BlockSpec(memory_space=pltpu.VMEM)
SMEM = pl.BlockSpec(memory_space=pltpu.SMEM)
ANY = pl.BlockSpec(memory_space=pl.ANY)
MIB = 1024 * 1024


def params(mib):
    return pltpu.CompilerParams(vmem_limit_bytes=mib * MIB)


CHEAP = pl.CostEstimate(flops=1, bytes_accessed=1, transcendentals=0)


def OUT(size, dtype):
    return pltpu.VMEM(size, dtype)


def dot_t(left, right):
    return lax.dot_general(
        left, right, (((1,), (1,)), ((), ())), preferred_element_type=jnp.float32
    )


def power6(product, samples):
    half = (1.0 + product * (1.0 / samples)) * 0.5
    square = half * half
    return square * square * square


def standard_kernel(x_ref, z_ref, za_ref, zb_ref):
    x = x_ref[...]
    centered = x - jnp.mean(x, axis=1, keepdims=True)
    spread = jnp.mean(centered * centered, axis=1, keepdims=True)
    z = (centered * lax.rsqrt(spread + 1e-06)).astype(jnp.bfloat16)
    z_ref[...] = z
    wa = za_ref.shape[1]
    za_ref[...] = z[:, :wa]
    zb_ref[...] = z[:, wa:]


def select_kernel(n, hot_ref, *refs):
    shards, (mine_ref, theirs_ref) = refs[:n], refs[n:]
    half = mine_ref.shape[0]
    genes = jnp.concatenate([s[...] for s in shards], axis=0)
    for out, at in ((mine_ref, 0), (theirs_ref, half)):
        out[...] = jnp.dot(
            hot_ref[at : at + half, :], genes, preferred_element_type=jnp.float32
        ).astype(jnp.bfloat16)


def direct_kernel(n, m, cols_ref, kr_ref, kc_ref, *refs):
    refs = list(refs)
    take = lambda count: [refs.pop(0) for _ in range(count)]
    za, zb, pieces = take(n), take(n), take(m)
    zr, zc, inverse, share = refs
    local, samples = pieces[0].shape
    wa = za[0].shape[1]
    for j in range(n):
        at = pl.ds(pl.multiple_of(cols_ref[j] * local, local), local)
        zr[at, :wa] = za[j][...]
        zr[at, wa:] = zb[j][...]
    for i in range(m):
        at = pl.ds(pl.multiple_of(cols_ref[n + i] * local, local), local)
        zc[at, :] = pieces[i][...]
    block = 2 * local
    for b in range(n * local // block):
        rows = slice(b * block, (b + 1) * block)
        direct = power6(dot_t(zr[rows, :], zc[...]), samples)
        inv = 1.0 / (jnp.minimum(kr_ref[rows, :], kc_ref[...]) + 1.0 - direct)
        inverse[rows, :] = inv
        share[rows, :] = direct * inv


def products(left, pa, pb):
    wa = pa.shape[1]
    return dot_t(left[:, :wa], pa[...]) + dot_t(left[:, wa:], pb[...])


def partial_kernel(zr, zc, pa, pb, row_part, col_part):
    row_part[...] = products(zr[...], pa, pb)
    col_part[...] = products(zc[...], pa, pb)


def final_kernel(zr, zc, pa, pb, row_part, col_part, inverse, share, out_ref, stage, sems):
    height, samples = zr.shape

    def both(part, left):
        product = jnp.concatenate([part, products(left, pa, pb)], axis=1)
        return power6(product, samples).astype(jnp.bfloat16)

    acol = both(col_part[...], zc[...])
    count = sems.shape[0]
    block = height // count
    copies = []
    for b in range(count):
        rows = slice(b * block, (b + 1) * block)
        arow = both(row_part[rows, :], zr[rows, :])
        stage[rows, :] = dot_t(arow, acol) * inverse[rows, :] + share[rows, :]
        copy = pltpu.make_async_copy(
            stage.at[rows, :], out_ref.at[rows, :], sems.at[b]
        )
        copy.start()
        copies.append(copy)
    for copy in copies:
        copy.wait()


def add_kernel(left, right, out):
    out[...] = left[...] + right[...]


def add(left, right):
    return pl.pallas_call(
        add_kernel,
        out_shape=OUT(left.shape, left.dtype),
        in_specs=[VMEM] * 2,
        out_specs=VMEM,
        compiler_params=params(4),
        cost_estimate=CHEAP,
        name="add",
    )(left, right)


def sum_part_kernel(side_ref, left, right, both, part):
    total = left[...] + right[...]
    both[...] = total
    rows = part.shape[0]

    @pl.when(side_ref[0] == 0)
    def _():
        part[...] = total[:rows, :]

    @pl.when(side_ref[0] != 0)
    def _():
        part[...] = total[rows:, :]


def merge_kernel(side_ref, sum_a, got_a, sum_b, mine, mate, out_a, out_b):
    out_a[...] = sum_a[...] + got_a[...]
    rows = mine.shape[0]
    for side in range(2):
        first, second = (mine, mate) if side == 0 else (mate, mine)

        @pl.when(side_ref[0] == side)
        def _():
            out_b[:rows, :] = sum_b[:rows, :] + first[...]
            out_b[rows:, :] = sum_b[rows:, :] + second[...]


def per_device(expression, pivots, degrees):
    n_rows = lax.axis_size("rows")
    n = lax.axis_size("cols")
    r = lax.axis_index("rows")
    c = lax.axis_index("cols")
    local, samples = expression.shape
    wa = samples // 2
    wb = samples - wa
    bf16 = jnp.bfloat16

    z, za, zb = pl.pallas_call(
        standard_kernel,
        out_shape=[
            jax.ShapeDtypeStruct((local, samples), bf16),
            jax.ShapeDtypeStruct((local, wa), bf16),
            jax.ShapeDtypeStruct((local, wb), bf16),
        ],
        in_specs=[VMEM],
        out_specs=[VMEM] * 3,
        compiler_params=params(8),
        name="standardize",
    )(expression)

    order = list(range(0, n, 2)) + list(range(n - 1, 0, -2))
    forward = [(order[k], order[(k + 1) % n]) for k in range(n)]
    backward = [(b, a) for a, b in forward]
    flip = lambda v, mask: lax.ppermute(
        v, "rows", [(i, i ^ mask) for i in range(n_rows)]
    )

    offsets = [0]
    for s in range(1, n // 2 + 1):
        offsets += [-s, s] if s < n // 2 else [s]
    height = n * local
    scale = degrees.astype(jnp.float32) * (1.0 / 1024.0)
    kc = lax.dynamic_index_in_dim(scale.reshape(n_rows, n, local), c, 1, False).reshape(1, -1)
    kr = lax.dynamic_slice_in_dim(scale, r * height, height, 0).reshape(-1, 1)
    fa, ba, fb, bb = za, za, zb, zb
    list_a, list_b = [za], [zb]
    top = n_rows // 2
    across = flip(z, top)
    for s in range(1, n // 2 + 1):
        last = s == n // 2
        if s == n // 2 - 1:
            fb, across, kr, kc = lax.optimization_barrier((fb, across, kr, kc))
        fa = lax.ppermute(fa, "cols", forward)
        list_a.append(fa)
        if not last:
            ba = lax.ppermute(ba, "cols", backward)
            list_a.append(ba)
            fb = lax.ppermute(fb, "cols", forward)
            list_b.append(fb)
        bb = lax.ppermute(bb, "cols", backward)
        list_b.append(bb)

    place = jnp.where(c % 2 == 0, c // 2, n - 1 - c // 2)
    spots = (place + jnp.array(offsets, jnp.int32)) % n
    columns = jnp.where(spots < n // 2, 2 * spots, 2 * (n - 1 - spots) + 1)
    ids = ((r * n + columns)[:, None] * local + jnp.arange(local, dtype=jnp.int32)).reshape(-1)
    gathered = lax.optimization_barrier((*list_a, *list_b))
    list_a, list_b = gathered[:n], gathered[n:]
    half = pivots.shape[0] // 2
    side = r % 2
    split = pivots.reshape(2, half)
    ordered = jnp.concatenate(
        [
            lax.dynamic_index_in_dim(split, side, 0, False),
            lax.dynamic_index_in_dim(split, 1 - side, 0, False),
        ]
    )
    hot = (ordered[:, None] == ids[None, :]).astype(bf16)

    def pivot_sums(shards):
        width = shards[0].shape[1]
        mine, theirs = pl.pallas_call(
            functools.partial(select_kernel, n),
            out_shape=[jax.ShapeDtypeStruct((half, width), bf16)] * 2,
            in_specs=[VMEM] * (n + 1),
            out_specs=[VMEM] * 2,
            compiler_params=params(8),
            cost_estimate=CHEAP,
            name="select",
        )(hot, *shards)
        return mine, flip(theirs, 1)

    parity = (c % 2).astype(jnp.int32).reshape(1)
    beside = [(k, k ^ 1) for k in range(n)]
    mine, theirs = pivot_sums(list_b)
    sum_b, part = pl.pallas_call(
        sum_part_kernel,
        out_shape=[OUT(mine.shape, bf16), OUT((half // 2, mine.shape[1]), bf16)],
        in_specs=[SMEM, VMEM, VMEM],
        out_specs=[VMEM] * 2,
        compiler_params=params(4),
        cost_estimate=CHEAP,
        name="sum",
    )(parity, mine, theirs)
    got_b = flip(part, top)
    sum_a = add(*pivot_sums(list_a))
    sum_a, z, across = lax.optimization_barrier((sum_a, z, across))
    got_a = flip(sum_a, top)
    mate_b = lax.ppermute(got_b, "cols", beside)
    pieces, masks = [z, across], [0, top]
    mask = top // 2
    while mask:
        pieces += [flip(p, mask) for p in pieces]
        masks += [q ^ mask for q in masks]
        mask //= 2

    where = jnp.concatenate([columns, jnp.array(masks, jnp.int32) ^ r])
    width = n_rows * local
    f32 = jnp.float32
    shape = jax.ShapeDtypeStruct
    zr, zc, inverse, share = pl.pallas_call(
        functools.partial(direct_kernel, n, n_rows),
        out_shape=[
            shape((height, samples), bf16),
            shape((width, samples), bf16),
            shape((height, width), f32),
            shape((height, width), f32),
        ],
        in_specs=[SMEM] + [VMEM] * (2 + 2 * n + n_rows),
        out_specs=[VMEM] * 4,
        compiler_params=params(8),
        cost_estimate=CHEAP,
        name="direct",
    )(where, kr, kc, *list_a, *list_b, *pieces)
    got_a, got_b, zr, zc, inverse, share, mate_b = lax.optimization_barrier(
        (got_a, got_b, zr, zc, inverse, share, mate_b)
    )
    total_a, total_b = pl.pallas_call(
        merge_kernel,
        out_shape=[OUT(sum_a.shape, bf16), OUT(sum_b.shape, bf16)],
        in_specs=[SMEM] + [VMEM] * 5,
        out_specs=[VMEM] * 2,
        compiler_params=params(4),
        cost_estimate=CHEAP,
        name="merge",
    )(parity, sum_a, got_a, sum_b, got_b, mate_b)
    far_a, far_b = flip(total_a, 1), flip(total_b, 1)
    row_part, col_part = pl.pallas_call(
        partial_kernel,
        out_shape=[shape((height, half), f32), shape((width, half), f32)],
        in_specs=[VMEM] * 4,
        out_specs=[VMEM] * 2,
        compiler_params=params(8),
        cost_estimate=CHEAP,
        name="partial",
    )(zr, zc, total_a, total_b)
    return pl.pallas_call(
        final_kernel,
        out_shape=shape((height, width), f32),
        in_specs=[VMEM] * 8,
        out_specs=ANY,
        scratch_shapes=[pltpu.VMEM((height, width), f32), pltpu.SemaphoreType.DMA((n // 2,))],
        compiler_params=params(16),
        cost_estimate=CHEAP,
        name="final",
    )(zr, zc, far_a, far_b, row_part, col_part, inverse, share)


def solution(mesh):
    in_specs = (P(("rows", "cols"), None), P(), P())
    out_specs = P("rows", "cols")
    return jax.shard_map(
        per_device, mesh=mesh, in_specs=in_specs, out_specs=out_specs, check_vma=False
    )
```

```python
import functools

import jax
import jax.numpy as jnp
from jax import lax
from jax.experimental import pallas as pl
from jax.experimental.pallas import tpu as pltpu
from jax.sharding import PartitionSpec as P

VMEM = pl.BlockSpec(memory_space=pltpu.VMEM)
SMEM = pl.BlockSpec(memory_space=pltpu.SMEM)
ANY = pl.BlockSpec(memory_space=pl.ANY)
MIB = 1024 * 1024


def params(mib):
    return pltpu.CompilerParams(vmem_limit_bytes=mib * MIB)


CHEAP = pl.CostEstimate(flops=1, bytes_accessed=1, transcendentals=0)


def OUT(size, dtype):
    return pltpu.VMEM(size, dtype)


def dot_t(left, right):
    return lax.dot_general(
        left, right, (((1,), (1,)), ((), ())), preferred_element_type=jnp.float32
    )


def power6(product, samples):
    half = (1.0 + product * (1.0 / samples)) * 0.5
    square = half * half
    return square * square * square


def standard_kernel(x_ref, z_ref, za_ref, zb_ref):
    x = x_ref[...]
    centered = x - jnp.mean(x, axis=1, keepdims=True)
    spread = jnp.mean(centered * centered, axis=1, keepdims=True)
    z = (centered * lax.rsqrt(spread + 1e-06)).astype(jnp.bfloat16)
    z_ref[...] = z
    wa = za_ref.shape[1]
    za_ref[...] = z[:, :wa]
    zb_ref[...] = z[:, wa:]


def select_kernel(n, hot_ref, *refs):
    shards, (mine_ref, theirs_ref) = refs[:n], refs[n:]
    half = mine_ref.shape[0]
    genes = jnp.concatenate([s[...] for s in shards], axis=0)
    for out, at in ((mine_ref, 0), (theirs_ref, half)):
        out[...] = jnp.dot(
            hot_ref[at : at + half, :], genes, preferred_element_type=jnp.float32
        ).astype(jnp.bfloat16)


def direct_kernel(n, m, cols_ref, kr_ref, kc_ref, *refs):
    refs = list(refs)
    take = lambda count: [refs.pop(0) for _ in range(count)]
    za, zb, pieces = take(n), take(n), take(m)
    zr, zc, inverse, share = refs
    local, samples = pieces[0].shape
    wa = za[0].shape[1]
    for j in range(n):
        at = pl.ds(pl.multiple_of(cols_ref[j] * local, local), local)
        zr[at, :wa] = za[j][...]
        zr[at, wa:] = zb[j][...]
    for i in range(m):
        at = pl.ds(pl.multiple_of(cols_ref[n + i] * local, local), local)
        zc[at, :] = pieces[i][...]
    block = 2 * local
    for b in range(n * local // block):
        rows = slice(b * block, (b + 1) * block)
        direct = power6(dot_t(zr[rows, :], zc[...]), samples)
        inv = 1.0 / (jnp.minimum(kr_ref[rows, :], kc_ref[...]) + 1.0 - direct)
        inverse[rows, :] = inv
        share[rows, :] = direct * inv


def products(left, rows):
    return dot_t(left, rows[...])


def partial_kernel(zr, zc, near, row_part, col_part):
    row_part[...] = products(zr[...], near)
    col_part[...] = products(zc[...], near)


def final_kernel(zr, zc, far, row_part, col_part, inverse, share, out_ref, stage, sems):
    height, samples = zr.shape

    def both(part, left):
        product = jnp.concatenate([part, products(left, far)], axis=1)
        return power6(product, samples).astype(jnp.bfloat16)

    acol = both(col_part[...], zc[...])
    count = sems.shape[0]
    block = height // count
    copies = []
    for b in range(count):
        rows = slice(b * block, (b + 1) * block)
        arow = both(row_part[rows, :], zr[rows, :])
        stage[rows, :] = dot_t(arow, acol) * inverse[rows, :] + share[rows, :]
        copy = pltpu.make_async_copy(
            stage.at[rows, :], out_ref.at[rows, :], sems.at[b]
        )
        copy.start()
        copies.append(copy)
    for copy in copies:
        copy.wait()


def add_kernel(left, right, out):
    out[...] = left[...] + right[...]


def add(left, right):
    return pl.pallas_call(
        add_kernel,
        out_shape=OUT(left.shape, left.dtype),
        in_specs=[VMEM] * 2,
        out_specs=VMEM,
        compiler_params=params(4),
        cost_estimate=CHEAP,
        name="add",
    )(left, right)


def sum_part_kernel(side_ref, left, right, both, part):
    total = left[...] + right[...]
    both[...] = total
    rows = part.shape[0]

    @pl.when(side_ref[0] == 0)
    def _():
        part[...] = total[:rows, :]

    @pl.when(side_ref[0] != 0)
    def _():
        part[...] = total[rows:, :]


def merge_kernel(side_ref, sum_a, got_a, sum_b, mine, mate, out):
    wa = sum_a.shape[1]
    out[:, :wa] = sum_a[...] + got_a[...]
    rows = mine.shape[0]
    for side in range(2):
        first, second = (mine, mate) if side == 0 else (mate, mine)

        @pl.when(side_ref[0] == side)
        def _():
            out[:rows, wa:] = sum_b[:rows, :] + first[...]
            out[rows:, wa:] = sum_b[rows:, :] + second[...]


def per_device(expression, pivots, degrees):
    n_rows = lax.axis_size("rows")
    n = lax.axis_size("cols")
    r = lax.axis_index("rows")
    c = lax.axis_index("cols")
    local, samples = expression.shape
    wa = samples // 2
    wb = samples - wa
    bf16 = jnp.bfloat16

    z, za, zb = pl.pallas_call(
        standard_kernel,
        out_shape=[
            jax.ShapeDtypeStruct((local, samples), bf16),
            jax.ShapeDtypeStruct((local, wa), bf16),
            jax.ShapeDtypeStruct((local, wb), bf16),
        ],
        in_specs=[VMEM],
        out_specs=[VMEM] * 3,
        compiler_params=params(8),
        name="standardize",
    )(expression)

    order = list(range(0, n, 2)) + list(range(n - 1, 0, -2))
    forward = [(order[k], order[(k + 1) % n]) for k in range(n)]
    backward = [(b, a) for a, b in forward]
    flip = lambda v, mask: lax.ppermute(
        v, "rows", [(i, i ^ mask) for i in range(n_rows)]
    )

    offsets = [0]
    for s in range(1, n // 2 + 1):
        offsets += [-s, s] if s < n // 2 else [s]
    height = n * local
    scale = degrees.astype(jnp.float32) * (1.0 / 1024.0)
    kc = lax.dynamic_index_in_dim(scale.reshape(n_rows, n, local), c, 1, False).reshape(1, -1)
    kr = lax.dynamic_slice_in_dim(scale, r * height, height, 0).reshape(-1, 1)
    fa, ba, fb, bb = za, za, zb, zb
    list_a, list_b = [za], [zb]
    top = n_rows // 2
    across = flip(z, top)
    for s in range(1, n // 2 + 1):
        last = s == n // 2
        if s == n // 2 - 1:
            fb, across, kr, kc = lax.optimization_barrier((fb, across, kr, kc))
        fa = lax.ppermute(fa, "cols", forward)
        list_a.append(fa)
        if not last:
            ba = lax.ppermute(ba, "cols", backward)
            list_a.append(ba)
            fb = lax.ppermute(fb, "cols", forward)
            list_b.append(fb)
        bb = lax.ppermute(bb, "cols", backward)
        list_b.append(bb)

    place = jnp.where(c % 2 == 0, c // 2, n - 1 - c // 2)
    spots = (place + jnp.array(offsets, jnp.int32)) % n
    columns = jnp.where(spots < n // 2, 2 * spots, 2 * (n - 1 - spots) + 1)
    ids = ((r * n + columns)[:, None] * local + jnp.arange(local, dtype=jnp.int32)).reshape(-1)
    gathered = lax.optimization_barrier((*list_a, *list_b))
    list_a, list_b = gathered[:n], gathered[n:]
    half = pivots.shape[0] // 2
    side = r % 2
    split = pivots.reshape(2, half)
    ordered = jnp.concatenate(
        [
            lax.dynamic_index_in_dim(split, side, 0, False),
            lax.dynamic_index_in_dim(split, 1 - side, 0, False),
        ]
    )
    hot = (ordered[:, None] == ids[None, :]).astype(bf16)

    def pivot_sums(shards):
        width = shards[0].shape[1]
        mine, theirs = pl.pallas_call(
            functools.partial(select_kernel, n),
            out_shape=[jax.ShapeDtypeStruct((half, width), bf16)] * 2,
            in_specs=[VMEM] * (n + 1),
            out_specs=[VMEM] * 2,
            compiler_params=params(8),
            cost_estimate=CHEAP,
            name="select",
        )(hot, *shards)
        return mine, flip(theirs, 1)

    parity = (c % 2).astype(jnp.int32).reshape(1)
    beside = [(k, k ^ 1) for k in range(n)]
    mine, theirs = pivot_sums(list_b)
    sum_b, part = pl.pallas_call(
        sum_part_kernel,
        out_shape=[OUT(mine.shape, bf16), OUT((half // 2, mine.shape[1]), bf16)],
        in_specs=[SMEM, VMEM, VMEM],
        out_specs=[VMEM] * 2,
        compiler_params=params(4),
        cost_estimate=CHEAP,
        name="sum",
    )(parity, mine, theirs)
    got_b = flip(part, top)
    sum_a = add(*pivot_sums(list_a))
    sum_a, z, across = lax.optimization_barrier((sum_a, z, across))
    got_a = flip(sum_a, top)
    mate_b = lax.ppermute(got_b, "cols", beside)
    pieces, masks = [z, across], [0, top]
    mask = top // 2
    while mask:
        pieces += [flip(p, mask) for p in pieces]
        masks += [q ^ mask for q in masks]
        mask //= 2

    where = jnp.concatenate([columns, jnp.array(masks, jnp.int32) ^ r])
    width = n_rows * local
    f32 = jnp.float32
    shape = jax.ShapeDtypeStruct
    zr, zc, inverse, share = pl.pallas_call(
        functools.partial(direct_kernel, n, n_rows),
        out_shape=[
            shape((height, samples), bf16),
            shape((width, samples), bf16),
            shape((height, width), f32),
            shape((height, width), f32),
        ],
        in_specs=[SMEM] + [VMEM] * (2 + 2 * n + n_rows),
        out_specs=[VMEM] * 4,
        compiler_params=params(8),
        cost_estimate=CHEAP,
        name="direct",
    )(where, kr, kc, *list_a, *list_b, *pieces)
    got_a, got_b, zr, zc, inverse, share, mate_b = lax.optimization_barrier(
        (got_a, got_b, zr, zc, inverse, share, mate_b)
    )
    total = pl.pallas_call(
        merge_kernel,
        out_shape=OUT((half, samples), bf16),
        in_specs=[SMEM] + [VMEM] * 5,
        out_specs=VMEM,
        compiler_params=params(4),
        cost_estimate=CHEAP,
        name="merge",
    )(parity, sum_a, got_a, sum_b, got_b, mate_b)
    far = flip(total, 1)
    row_part, col_part = pl.pallas_call(
        partial_kernel,
        out_shape=[shape((height, half), f32), shape((width, half), f32)],
        in_specs=[VMEM] * 3,
        out_specs=[VMEM] * 2,
        compiler_params=params(8),
        cost_estimate=CHEAP,
        name="partial",
    )(zr, zc, total)
    return pl.pallas_call(
        final_kernel,
        out_shape=shape((height, width), f32),
        in_specs=[VMEM] * 7,
        out_specs=ANY,
        scratch_shapes=[pltpu.VMEM((height, width), f32), pltpu.SemaphoreType.DMA((n // 2,))],
        compiler_params=params(16),
        cost_estimate=CHEAP,
        name="final",
    )(zr, zc, far, row_part, col_part, inverse, share)


def solution(mesh):
    in_specs = (P(("rows", "cols"), None), P(), P())
    out_specs = P("rows", "cols")
    return jax.shard_map(
        per_device, mesh=mesh, in_specs=in_specs, out_specs=out_specs, check_vma=False
    )
```

```python
import functools

import jax
import jax.numpy as jnp
from jax import lax
from jax.experimental import pallas as pl
from jax.experimental.pallas import tpu as pltpu
from jax.sharding import PartitionSpec as P

VMEM = pl.BlockSpec(memory_space=pltpu.VMEM)
SMEM = pl.BlockSpec(memory_space=pltpu.SMEM)
ANY = pl.BlockSpec(memory_space=pl.ANY)
MIB = 1024 * 1024


def params(mib):
    return pltpu.CompilerParams(vmem_limit_bytes=mib * MIB)


CHEAP = pl.CostEstimate(flops=1, bytes_accessed=1, transcendentals=0)


def OUT(size, dtype):
    return pltpu.VMEM(size, dtype)


def dot_t(left, right):
    return lax.dot_general(
        left, right, (((1,), (1,)), ((), ())), preferred_element_type=jnp.float32
    )


def power6(product, samples):
    half = (1.0 + product * (1.0 / samples)) * 0.5
    square = half * half
    return square * square * square


def standard_kernel(x_ref, z_ref, za_ref, zb_ref):
    x = x_ref[...]
    centered = x - jnp.mean(x, axis=1, keepdims=True)
    spread = jnp.mean(centered * centered, axis=1, keepdims=True)
    z = (centered * lax.rsqrt(spread + 1e-06)).astype(jnp.bfloat16)
    z_ref[...] = z
    wa = za_ref.shape[1]
    za_ref[...] = z[:, :wa]
    zb_ref[...] = z[:, wa:]


def select_kernel(n, hot_ref, *refs):
    shards, (mine_ref, theirs_ref) = refs[:n], refs[n:]
    half = mine_ref.shape[0]
    genes = jnp.concatenate([s[...] for s in shards], axis=0)
    for out, at in ((mine_ref, 0), (theirs_ref, half)):
        out[...] = jnp.dot(
            hot_ref[at : at + half, :], genes, preferred_element_type=jnp.float32
        ).astype(jnp.bfloat16)


def direct_kernel(n, m, cols_ref, kr_ref, kc_ref, *refs):
    refs = list(refs)
    take = lambda count: [refs.pop(0) for _ in range(count)]
    za, zb, pieces = take(n), take(n), take(m)
    zr, zc, inverse, share = refs
    local, samples = pieces[0].shape
    wa = za[0].shape[1]
    for j in range(n):
        at = pl.ds(pl.multiple_of(cols_ref[j] * local, local), local)
        zr[at, :wa] = za[j][...]
        zr[at, wa:] = zb[j][...]
    for i in range(m):
        at = pl.ds(pl.multiple_of(cols_ref[n + i] * local, local), local)
        zc[at, :] = pieces[i][...]
    block = 2 * local
    for b in range(n * local // block):
        rows = slice(b * block, (b + 1) * block)
        direct = power6(dot_t(zr[rows, :], zc[...]), samples)
        inv = 1.0 / (jnp.minimum(kr_ref[rows, :], kc_ref[...]) + 1.0 - direct)
        inverse[rows, :] = inv
        share[rows, :] = direct * inv


def products(left, rows):
    return dot_t(left, rows[...])


def partial_kernel(zr, zc, near, row_part, col_part):
    row_part[...] = products(zr[...], near)
    col_part[...] = products(zc[...], near)


def final_kernel(zr, zc, far, row_part, col_part, inverse, share, out_ref, stage, sems):
    height, samples = zr.shape

    def both(part, left):
        product = jnp.concatenate([part, products(left, far)], axis=1)
        return power6(product, samples).astype(jnp.bfloat16)

    acol = both(col_part[...], zc[...])
    count = sems.shape[0]
    block = height // count
    copies = []
    for b in range(count):
        rows = slice(b * block, (b + 1) * block)
        arow = both(row_part[rows, :], zr[rows, :])
        stage[rows, :] = dot_t(arow, acol) * inverse[rows, :] + share[rows, :]
        copy = pltpu.make_async_copy(
            stage.at[rows, :], out_ref.at[rows, :], sems.at[b]
        )
        copy.start()
        copies.append(copy)
    for copy in copies:
        copy.wait()


def add_kernel(left, right, out):
    out[...] = left[...] + right[...]


def add(left, right):
    return pl.pallas_call(
        add_kernel,
        out_shape=OUT(left.shape, left.dtype),
        in_specs=[VMEM] * 2,
        out_specs=VMEM,
        compiler_params=params(4),
        cost_estimate=CHEAP,
        name="add",
    )(left, right)


def sum_part_kernel(side_ref, left, right, both, part):
    total = left[...] + right[...]
    both[...] = total
    rows = part.shape[0]

    @pl.when(side_ref[0] == 0)
    def _():
        part[...] = total[:rows, :]

    @pl.when(side_ref[0] != 0)
    def _():
        part[...] = total[rows:, :]


def merge_kernel(side_ref, sum_a, got_a, sum_b, mine, mate, out):
    wa = sum_a.shape[1]
    out[:, :wa] = sum_a[...] + got_a[...]
    rows = mine.shape[0]
    for side in range(2):
        first, second = (mine, mate) if side == 0 else (mate, mine)

        @pl.when(side_ref[0] == side)
        def _():
            out[:rows, wa:] = sum_b[:rows, :] + first[...]
            out[rows:, wa:] = sum_b[rows:, :] + second[...]


def per_device(expression, pivots, degrees):
    n_rows = lax.axis_size("rows")
    n = lax.axis_size("cols")
    r = lax.axis_index("rows")
    c = lax.axis_index("cols")
    local, samples = expression.shape
    wa = samples // 2
    wb = samples - wa
    bf16 = jnp.bfloat16

    z, za, zb = pl.pallas_call(
        standard_kernel,
        out_shape=[
            jax.ShapeDtypeStruct((local, samples), bf16),
            jax.ShapeDtypeStruct((local, wa), bf16),
            jax.ShapeDtypeStruct((local, wb), bf16),
        ],
        in_specs=[VMEM],
        out_specs=[VMEM] * 3,
        compiler_params=params(8),
        name="standardize",
    )(expression)

    order = list(range(0, n, 2)) + list(range(n - 1, 0, -2))
    forward = [(order[k], order[(k + 1) % n]) for k in range(n)]
    backward = [(b, a) for a, b in forward]
    flip = lambda v, mask: lax.ppermute(
        v, "rows", [(i, i ^ mask) for i in range(n_rows)]
    )

    offsets = [0]
    for s in range(1, n // 2 + 1):
        offsets += [-s, s] if s < n // 2 else [s]
    height = n * local
    scale = degrees.astype(jnp.float32) * (1.0 / 1024.0)
    kc = lax.dynamic_index_in_dim(scale.reshape(n_rows, n, local), c, 1, False).reshape(1, -1)
    kr = lax.dynamic_slice_in_dim(scale, r * height, height, 0).reshape(-1, 1)
    fa, ba, fb, bb = za, za, zb, zb
    list_a, list_b = [za], [zb]
    top = n_rows // 2
    across = flip(z, top)
    for s in range(1, n // 2 + 1):
        last = s == n // 2
        if s == n // 2 - 1:
            fb, across, kr, kc = lax.optimization_barrier((fb, across, kr, kc))
        fa = lax.ppermute(fa, "cols", forward)
        list_a.append(fa)
        if not last:
            ba = lax.ppermute(ba, "cols", backward)
            list_a.append(ba)
            fb = lax.ppermute(fb, "cols", forward)
            list_b.append(fb)
        bb = lax.ppermute(bb, "cols", backward)
        list_b.append(bb)

    place = jnp.where(c % 2 == 0, c // 2, n - 1 - c // 2)
    spots = (place + jnp.array(offsets, jnp.int32)) % n
    columns = jnp.where(spots < n // 2, 2 * spots, 2 * (n - 1 - spots) + 1)
    ids = ((r * n + columns)[:, None] * local + jnp.arange(local, dtype=jnp.int32)).reshape(-1)
    gathered = lax.optimization_barrier((*list_a, *list_b))
    list_a, list_b = gathered[:n], gathered[n:]
    half = pivots.shape[0] // 2
    side = r % 2
    split = pivots.reshape(2, half)
    ordered = jnp.concatenate(
        [
            lax.dynamic_index_in_dim(split, side, 0, False),
            lax.dynamic_index_in_dim(split, 1 - side, 0, False),
        ]
    )
    hot = (ordered[:, None] == ids[None, :]).astype(bf16)

    def pivot_sums(shards):
        width = shards[0].shape[1]
        mine, theirs = pl.pallas_call(
            functools.partial(select_kernel, n),
            out_shape=[jax.ShapeDtypeStruct((half, width), bf16)] * 2,
            in_specs=[VMEM] * (n + 1),
            out_specs=[VMEM] * 2,
            compiler_params=params(8),
            cost_estimate=CHEAP,
            name="select",
        )(hot, *shards)
        return mine, flip(theirs, 1)

    parity = (c % 2).astype(jnp.int32).reshape(1)
    beside = [(k, k ^ 1) for k in range(n)]
    mine, theirs = pivot_sums(list_b)
    sum_b, part = pl.pallas_call(
        sum_part_kernel,
        out_shape=[OUT(mine.shape, bf16), OUT((half // 2, mine.shape[1]), bf16)],
        in_specs=[SMEM, VMEM, VMEM],
        out_specs=[VMEM] * 2,
        compiler_params=params(4),
        cost_estimate=CHEAP,
        name="sum",
    )(parity, mine, theirs)
    got_b = flip(part, top)
    sum_a = add(*pivot_sums(list_a))
    part, z, across = lax.optimization_barrier((part, z, across))
    got_a = flip(sum_a, top)
    mate_b = lax.ppermute(got_b, "cols", beside)
    pieces, masks = [z, across], [0, top]
    mask = top // 2
    while mask:
        pieces += [flip(p, mask) for p in pieces]
        masks += [q ^ mask for q in masks]
        mask //= 2

    where = jnp.concatenate([columns, jnp.array(masks, jnp.int32) ^ r])
    width = n_rows * local
    f32 = jnp.float32
    shape = jax.ShapeDtypeStruct
    zr, zc, inverse, share = pl.pallas_call(
        functools.partial(direct_kernel, n, n_rows),
        out_shape=[
            shape((height, samples), bf16),
            shape((width, samples), bf16),
            shape((height, width), f32),
            shape((height, width), f32),
        ],
        in_specs=[SMEM] + [VMEM] * (2 + 2 * n + n_rows),
        out_specs=[VMEM] * 4,
        compiler_params=params(8),
        cost_estimate=CHEAP,
        name="direct",
    )(where, kr, kc, *list_a, *list_b, *pieces)
    got_a, got_b, zr, zc, inverse, share, mate_b = lax.optimization_barrier(
        (got_a, got_b, zr, zc, inverse, share, mate_b)
    )
    total = pl.pallas_call(
        merge_kernel,
        out_shape=OUT((half, samples), bf16),
        in_specs=[SMEM] + [VMEM] * 5,
        out_specs=VMEM,
        compiler_params=params(4),
        cost_estimate=CHEAP,
        name="merge",
    )(parity, sum_a, got_a, sum_b, got_b, mate_b)
    far = flip(total, 1)
    row_part, col_part = pl.pallas_call(
        partial_kernel,
        out_shape=[shape((height, half), f32), shape((width, half), f32)],
        in_specs=[VMEM] * 3,
        out_specs=[VMEM] * 2,
        compiler_params=params(8),
        cost_estimate=CHEAP,
        name="partial",
    )(zr, zc, total)
    return pl.pallas_call(
        final_kernel,
        out_shape=shape((height, width), f32),
        in_specs=[VMEM] * 7,
        out_specs=ANY,
        scratch_shapes=[pltpu.VMEM((height, width), f32), pltpu.SemaphoreType.DMA((n // 2,))],
        compiler_params=params(16),
        cost_estimate=CHEAP,
        name="final",
    )(zr, zc, far, row_part, col_part, inverse, share)


def solution(mesh):
    in_specs = (P(("rows", "cols"), None), P(), P())
    out_specs = P("rows", "cols")
    return jax.shard_map(
        per_device, mesh=mesh, in_specs=in_specs, out_specs=out_specs, check_vma=False
    )
```
